32 devices in a mesh: dp: 8 (over z, y), tensor: 4 (over x, core).
Axes of the slice: x: 2, y: 2, z: 4, core: 2. Of those that a mesh axis runs over, the one named last changes fastest.
Arguments:
- block_input: bfloat16 [16, 1024, 1024], P('dp', 'tensor')
- attention_gain: float32 [1024], P('dp'), may hold values from 0.5 to 1.5
- attention_shift: float32 [1024], P('dp'), may hold values from -0.6 to 0.6
- feedforward_gain: float32 [1024], P('dp'), may hold values from 0.5 to 1.5
- feedforward_shift: float32 [1024], P('dp'), may hold values from -0.6 to 0.6
- projection: bfloat16 [1024, 3, 1024], P('dp', None, 'tensor'), may hold values from -0.1875 to 0.1875
- projection_bias: float32 [3, 1024], P(None, 'dp'), may hold values from -0.6 to 0.6
- mixing: bfloat16 [1024, 1024], P('tensor', 'dp'), may hold values from -0.75 to 0.75
- mixing_bias: float32 [1024], P('dp'), may hold values from -0.6 to 0.6
- expansion: bfloat16 [1024, 4096], P('dp', 'tensor'), may hold values from -0.1875 to 0.1875
- expansion_bias: float32 [4096], P('dp'), may hold values from -0.6 to 0.6
- reduction: bfloat16 [4096, 1024], P('tensor', 'dp'), may hold values from -0.09375 to 0.09375
- reduction_bias: float32 [1024], P('dp'), may hold values from -0.6 to 0.6
- segments: int32 [16, 1024], P('dp', 'tensor'), may hold values from 0 to 6, as said below
- cotangent: bfloat16 [16, 1024, 1024], P('dp', 'tensor'), may hold values from -6 to 6
Outputs:
- block_output: bfloat16 [16, 1024, 1024], P('dp', 'tensor')
- input_gradient: bfloat16 [16, 1024, 1024], P('dp', 'tensor')
- projection_gradient: float32 [1024, 3, 1024], P('dp', None, 'tensor')
- projection_bias_gradient: float32 [3, 1024], P(None, 'dp')
- mixing_gradient: float32 [1024, 1024], P('tensor', 'dp')
- mixing_bias_gradient: float32 [1024], P('dp')
- expansion_gradient: float32 [1024, 4096], P('dp', 'tensor')
- expansion_bias_gradient: float32 [4096], P('dp')
- reduction_gradient: float32 [4096, 1024], P('tensor', 'dp')
- reduction_bias_gradient: float32 [1024], P('dp')
- attention_gain_gradient: float32 [1024], P('dp')
- attention_shift_gradient: float32 [1024], P('dp')
- feedforward_gain_gradient: float32 [1024], P('dp')
- feedforward_shift_gradient: float32 [1024], P('dp')
The draws below stay inside these ranges and needn't reach their ends.
Inputs may be any that keep to these rules, and one draw needn't show every extreme that they name: `segments`: in each sequence of 1024 tokens the document numbers start at 0, never fall and rise by one where a new document begins; the first document may continue one begun in an earlier sequence. Before they are cut at a sequence's end, documents hold 204 to 2048 tokens. Of the 2 sequences of each index of dp, one, drawn from the seed, is a single document; where there are several, the next one after it (cyclically) holds a first piece of one token followed by documents of 204 tokens each.
All inputs are finite; a program needn't handle non-finite values.
Results may differ from the reference program's by a relative error of at most 0.009.
Values may be sent and summed in bfloat16 or wider, within the bound.
A program may use at most 128 MiB of HBM per device.

```python
import math
import jax
import jax.numpy as jnp
from jax import lax

D = 1024
H = 16
HD = 64
FF = 4096
SEQ = 1024
SEQ_DEV = 2
BATCH = 16


def draw_block_input(key, part):
    key = jax.random.fold_in(key, 5)
    keys = jax.random.split(key, 3)
    columns = jnp.exp(jax.random.uniform(keys[2], (1, 1, D), jnp.float32, -1.15, 1.15))
    base = jnp.clip(jax.random.normal(keys[0], (BATCH, SEQ, D), jnp.float32), -5.0, 5.0)
    rows = jnp.exp(jax.random.uniform(keys[1], (BATCH, SEQ, 1), jnp.float32, -1.15, 1.15))
    return (base * rows * columns).astype(jnp.bfloat16)


def draw_segments(key, part):
    key = jax.random.fold_in(key, 9)
    keys = jax.random.split(key, 3)
    shortest = max(SEQ // 5, 1)
    longest = 2 * SEQ
    pieces = SEQ // shortest + 2
    lengths = jax.random.randint(keys[0], (BATCH, pieces), shortest, longest + 1)
    consumed = jax.random.randint(keys[1], (BATCH,), 0, longest) % lengths[:, 0]
    chosen = jax.random.randint(keys[2], (BATCH // SEQ_DEV,), 0, SEQ_DEV)
    local_index = jnp.arange(BATCH) % SEQ_DEV
    single = local_index == jnp.repeat(chosen, SEQ_DEV)
    packed = (local_index == (jnp.repeat(chosen, SEQ_DEV) + 1) % SEQ_DEV) & jnp.logical_not(single)
    lengths = jnp.where(packed[:, None], shortest, lengths)
    leading = jnp.where(single, SEQ, jnp.where(packed, 1, lengths[:, 0] - consumed))
    lengths = lengths.at[:, 0].set(leading)
    ends = jnp.cumsum(lengths, axis=1)
    places = jnp.arange(SEQ)
    return jnp.sum((ends[:, None, :] <= places[None, :, None]).astype(jnp.int32), axis=2).astype(jnp.int32)


def spiked(entries, rng, source, target, blocks, factor):
    owner, partner = [(jnp.arange(entries.shape[axis_at]) // (entries.shape[axis_at] // blocks)).reshape([-1 if axis == axis_at else 1 for axis in range(entries.ndim)]) for axis_at in (source, target)]
    chosen = jax.random.permutation(rng, blocks)[partner]
    strong = (owner == chosen) | (owner == (partner + blocks // 2) % blocks)
    return jnp.where(strong, factor * entries, entries)


def levels(rng, shape, shards, least, high):
    level = 1.0
    for position, shards_of in shards:
        heights = jax.random.uniform(jax.random.fold_in(jax.random.fold_in(rng, 6), position), (shards_of,), jnp.float32, least / len(shards), high / len(shards))
        level = level * jnp.repeat(jnp.exp(heights), shape[position] // shards_of).reshape((-1,) + (1,) * (len(shape) - 1 - position))
    return level


def scatter_about(rng, extent, scale, limit, cuts=(), kind=jnp.bfloat16):
    loudness = levels(rng, extent, cuts, -0.22, 0.18) if cuts else 1.0
    values = jax.random.normal(rng, extent, jnp.float32) * scale * loudness
    return jnp.minimum(jnp.maximum(values, -limit), limit).astype(kind)


def noise_with(rng, shape, deviation, limit, shards, heavy, held_as=jnp.bfloat16):
    values = deviation * jax.random.normal(rng, shape, jnp.float32)
    if shards:
        values = values * levels(rng, shape, shards, -0.22, 0.18)
    return jnp.clip(spiked(values, jax.random.fold_in(rng, 3), *heavy), -limit, limit).astype(held_as)


def setup_inputs(seed: int = 0) -> dict:
    splits = jax.random.split(jax.random.key(seed), 16)
    return {
        "block_input": draw_block_input(jax.random.fold_in(splits[15], 71), 0),
        "attention_gain": jnp.clip(1.0 + 0.1 * jax.random.normal(splits[1], (D,), jnp.float32), 0.5, 1.5),
        "attention_shift": scatter_about(splits[2], (D,), 0.2, 0.6, ((0, 8),), jnp.float32),
        "feedforward_gain": jnp.clip(1.0 + 0.1 * jax.random.normal(splits[3], (D,), jnp.float32), 0.5, 1.5),
        "feedforward_shift": scatter_about(splits[4], (D,), 0.2, 0.6, ((0, 8),), jnp.float32),
        "projection": scatter_about(splits[5], (D, 3, D), D ** -0.5, 0.1875, ((0, 8), (2, 4))),
        "projection_bias": scatter_about(splits[6], (3, D), 0.2, 0.6, ((1, 8),), jnp.float32),
        "mixing": scatter_about(splits[7], (D, D), HD ** -0.5, 0.75, ((0, 4), (1, 8))),
        "mixing_bias": scatter_about(splits[8], (D,), 0.2, 0.6, ((0, 8),), jnp.float32),
        "expansion": scatter_about(splits[9], (D, FF), D ** -0.5, 0.1875, ((0, 8), (1, 4))),
        "expansion_bias": scatter_about(splits[10], (FF,), 0.2, 0.6, ((0, 8),), jnp.float32),
        "reduction": scatter_about(splits[11], (FF, D), FF ** -0.5, 0.09375, ((0, 4), (1, 8))),
        "reduction_bias": scatter_about(splits[12], (D,), 0.2, 0.6, ((0, 8),), jnp.float32),
        "segments": draw_segments(jax.random.fold_in(splits[15], 71), 0),
        "cotangent": noise_with(splits[14], (BATCH, SEQ, D), 1.0, 6.0, ((0, 8), (1, 4)), (0, 2, 8, 2.0)),
    }


EPS = 1e-05
MASKED = -1e+30
HIGHEST = lax.Precision.HIGHEST

@jax.custom_vjp
def low(v):
    return lax.optimization_barrier(v.astype(jnp.bfloat16)).astype(jnp.float32)

@jax.custom_vjp
def low_back(v):
    return v

def low_keep(v):
    return (low(v), None)

def low_pass(kept, grad):
    return (grad,)

def back_keep(v):
    return (v, None)

def back_low(kept, grad):
    return (low(grad),)
low.defvjp(low_keep, low_pass)
low_back.defvjp(back_keep, back_low)

def rotary_tables(length, head_size):
    half = head_size // 8
    freqs = 1.0 / 10000.0 ** (jnp.arange(half, dtype=jnp.float32) * 2.0 / (2 * half))
    angles = jnp.arange(length, dtype=jnp.float32)[:, None] * freqs[None, :]
    return (jnp.cos(angles), jnp.sin(angles))

def rotate(values, cosines, sines):
    half = cosines.shape[-1]
    front = values[..., :half]
    behind = values[..., half:2 * half]
    cosine_rows = cosines[:, None, :]
    sine_rows = sines[:, None, :]
    return jnp.concatenate([front * cosine_rows - behind * sine_rows, behind * cosine_rows + front * sine_rows, values[..., 2 * half:]], axis=-1)

def normalize(values, gains, offsets):
    average = lax.optimization_barrier(jnp.mean(values, axis=-1, keepdims=True))
    centered = values - average
    variance = lax.optimization_barrier(jnp.mean(centered * centered, axis=-1, keepdims=True))
    return centered * lax.rsqrt(variance + EPS) * gains + offsets

def attend_sequence(items):
    queries, keys, values, segment = items
    length = queries.shape[0]
    block = min(512, length)
    scale = queries.shape[-1] ** (-0.5)
    outputs = []
    for begin in range(0, length, block):
        stop = begin + block
        rows = begin + jnp.arange(block)
        columns = jnp.arange(stop)
        allowed = (segment[begin:stop][:, None] == segment[:stop][None, :]) & (columns[None, :] <= rows[:, None])
        scores = low_back(jnp.einsum('qhd,khd->hqk', queries[begin:stop], keys[:stop], precision=HIGHEST) * scale)
        scores = jnp.where(allowed[None], scores, MASKED)
        largest = lax.optimization_barrier(jnp.max(scores, axis=-1, keepdims=True))
        exponent = jnp.exp(scores - largest)
        probs = low(exponent / lax.optimization_barrier(jnp.sum(exponent, axis=-1, keepdims=True)))
        outputs.append(low(low_back(jnp.einsum('hqk,khd->qhd', probs, values[:stop], precision=HIGHEST))))
    return jnp.concatenate(outputs, axis=0)

def layer_forward(inputs, params, segments):
    gain_attention, shift_attention, gain_feedforward, shift_feedforward, projection, projection_bias, mixing, mixing_bias, expansion, expansion_bias, reduction, reduction_bias = params
    groups, length, width = inputs.shape
    first = low(normalize(inputs, gain_attention, shift_attention))
    second = low(normalize(inputs, gain_feedforward, shift_feedforward))
    heads_pre = low_back(jnp.einsum('gsd,dke->gske', first, projection, precision=HIGHEST) + projection_bias)
    split_heads = heads_pre.reshape(groups, length, 3, H, HD)
    cosines, sines = rotary_tables(length, HD)
    queries = low(rotate(split_heads[:, :, 0], cosines, sines))
    keys = low(rotate(split_heads[:, :, 1], cosines, sines))
    values = low(split_heads[:, :, 2])
    attended = lax.map(jax.checkpoint(attend_sequence), (queries, keys, values, segments)).reshape(groups, length, width)
    hidden_pre = low_back(jnp.einsum('gsd,df->gsf', second, expansion, precision=HIGHEST) + expansion_bias)
    activated = low(jax.nn.gelu(hidden_pre, approximate=False))
    branches = jnp.einsum('gse,ed->gsd', attended, mixing, precision=HIGHEST) + jnp.einsum('gsf,fd->gsd', activated, reduction, precision=HIGHEST)
    return inputs + branches + mixing_bias + reduction_bias

def reference(block_input, attention_gain, attention_shift, feedforward_gain, feedforward_shift, projection, projection_bias, mixing, mixing_bias, expansion, expansion_bias, reduction, reduction_bias, segments, cotangent):
    params = tuple((item.astype(jnp.float32) for item in (attention_gain, attention_shift, feedforward_gain, feedforward_shift, projection, projection_bias, mixing, mixing_bias, expansion, expansion_bias, reduction, reduction_bias)))
    group = math.gcd(BATCH, max(1, 4096 // SEQ))
    rounds = BATCH // group
    inputs = block_input.astype(jnp.float32).reshape(rounds, group, SEQ, D)
    grouped_segments = segments.reshape(rounds, group, SEQ)
    grouped_cotangent = cotangent.astype(jnp.float32).reshape(rounds, group, SEQ, D)

    def group_step(totals, items):
        group_input, group_segments, group_cotangent = items

        def forward(values, weights):
            return layer_forward(values, weights, group_segments)
        result, pullback = jax.vjp(forward, group_input, params)
        input_grad, param_grads = pullback(group_cotangent)
        totals = jax.tree.map(jnp.add, totals, param_grads)
        return (totals, (result.astype(jnp.bfloat16), input_grad.astype(jnp.bfloat16)))
    zeros = jax.tree.map(jnp.zeros_like, params)
    totals, (outputs, input_grads) = lax.scan(group_step, zeros, (inputs, grouped_segments, grouped_cotangent))
    return (outputs.reshape(BATCH, SEQ, D), input_grads.reshape(BATCH, SEQ, D), totals[4], totals[5], totals[6], totals[7], totals[8], totals[9], totals[10], totals[11], totals[0], totals[1], totals[2], totals[3])
```

```python
import numpy as np

import jax
import jax.numpy as jnp
from jax import lax
from jax.experimental import pallas as pl
from jax.experimental.pallas import tpu as pltpu
from jax.sharding import PartitionSpec as P

HD = 64
LANES = 128
EPS = 1e-05
MASKED = -1e30
F32 = jnp.float32
BF16 = jnp.bfloat16


def dot(left, right, left_dim, right_dim):
    return lax.dot_general(
        left, right, (((left_dim,), (right_dim,)), ((), ())), preferred_element_type=F32
    )


def rotary_lanes(length):
    half = HD // 8
    freqs = 1.0 / 10000.0 ** (np.arange(half, dtype=np.float32) * 2.0 / (2 * half))
    angles = np.arange(length, dtype=np.float32)[:, None] * freqs.astype(np.float32)[None, :]
    angles = angles.astype(np.float64)
    keep = np.ones((length, LANES), np.float32)
    from_below = np.zeros((length, LANES), np.float32)
    from_above = np.zeros((length, LANES), np.float32)
    for start in range(0, LANES, HD):
        keep[:, start : start + half] = np.cos(angles)
        keep[:, start + half : start + 2 * half] = np.cos(angles)
        from_above[:, start : start + half] = -np.sin(angles)
        from_below[:, start + half : start + 2 * half] = np.sin(angles)
    return keep, from_below, from_above


def attention_kernel(
    query_ref,
    key_ref,
    value_ref,
    query_bias,
    key_bias,
    value_bias,
    keep_ref,
    below_ref,
    above_ref,
    segment_column,
    segment_row,
    grad_ref,
    out_ref,
    heads_grad_ref,
    queries,
    keys,
    values,
    query_sum,
    key_sum,
    value_sum,
):
    length = query_ref.shape[1]
    block = min(256, length)
    half = HD // 8
    scale = HD**-0.5
    pair = pl.program_id(1)
    pair_count = pl.num_programs(1)

    def turn(data, sign):
        mixed = pltpu.roll(data, half, 1) * below_ref[...]
        mixed = mixed + pltpu.roll(data, LANES - half, 1) * above_ref[...]
        return data * keep_ref[...] + sign * mixed

    queries[...] = (turn(query_ref[0] + query_bias[...], 1.0)).astype(BF16) * BF16(scale)
    keys[...] = turn(key_ref[0] + key_bias[...], 1.0).astype(BF16)
    values[...] = (value_ref[0] + value_bias[...]).astype(BF16)
    key_sum[...] = jnp.zeros_like(key_sum)
    value_sum[...] = jnp.zeros_like(value_sum)
    for begin in range(0, length, block):
        stop = begin + block
        rows = lax.broadcasted_iota(jnp.int32, (block, stop), 0) + begin
        columns = lax.broadcasted_iota(jnp.int32, (block, stop), 1)
        allowed = (columns <= rows) & (
            segment_column[0, begin:stop, :] == segment_row[0, :, :stop]
        )
        out_block = jnp.zeros((block, LANES), F32)
        query_block = jnp.zeros((block, LANES), F32)
        for head in range(LANES // HD):

            def own(data):
                lane = lax.broadcasted_iota(jnp.int32, data.shape, 1)
                inside = (lane >= head * HD) & (lane < (head + 1) * HD)
                return jnp.where(inside, data.astype(F32), 0.0).astype(BF16)

            query = own(queries[begin:stop, :])
            grad = own(grad_ref[0, begin:stop, :])
            scores = jnp.where(allowed, dot(query, keys[:stop, :], 1, 1), MASKED)
            largest = jnp.max(scores, axis=1, keepdims=True)
            exponent = jnp.exp(scores - largest)
            probs = exponent * (1.0 / jnp.sum(exponent, axis=1, keepdims=True))
            rounded = probs.astype(BF16)
            out_block = out_block + dot(rounded, own(values[:stop, :]), 1, 0)
            prob_grad = dot(grad, values[:stop, :], 1, 1)
            delta = jnp.sum(prob_grad * probs, axis=1, keepdims=True)
            score_grad = (probs * (prob_grad - delta)).astype(BF16)
            query_block = query_block + dot(score_grad, own(keys[:stop, :]), 1, 0)
            key_sum[:stop, :] += dot(score_grad, query, 0, 0)
            value_sum[:stop, :] += dot(rounded, grad, 0, 0)
        out_ref[0, begin:stop, :] = out_block.astype(BF16)
        query_sum[begin:stop, :] = query_block * scale
    width = pair_count * LANES

    def place(index):
        return pl.ds(pl.multiple_of(index * width + pair * LANES, LANES), LANES)

    heads_grad_ref[0, :, place(0)] = turn(query_sum[...], -1.0).astype(BF16)
    heads_grad_ref[0, :, place(1)] = turn(key_sum[...], -1.0).astype(BF16)
    heads_grad_ref[0, :, place(2)] = value_sum[...].astype(BF16)


def attention(heads_pre, heads_bias, segment_rows, attended_grad):
    batch, length, columns = heads_pre.shape
    pairs = columns // (3 * LANES)
    keep, below, above = rotary_lanes(length)

    def part(index):
        return pl.BlockSpec((1, length, LANES), lambda b, p: (b, 0, index * pairs + p))

    def bias_part(index):
        return pl.BlockSpec((1, LANES), lambda b, p: (0, index * pairs + p))

    table = pl.BlockSpec((length, LANES), lambda b, p: (0, 0))
    piece = pl.BlockSpec((1, length, LANES), lambda b, p: (b, 0, p))
    area = batch * pairs * 2 * length * length * 5 // 8
    return pl.pallas_call(
        attention_kernel,
        grid=(batch, pairs),
        in_specs=[part(0), part(1), part(2), bias_part(0), bias_part(1), bias_part(2)]
        + [table] * 3
        + [
            pl.BlockSpec((1, length, 1), lambda b, p: (b, 0, 0)),
            pl.BlockSpec((1, 1, length), lambda b, p: (b, 0, 0)),
            piece,
        ],
        out_specs=[piece, pl.BlockSpec((1, length, columns), lambda b, p: (b, 0, 0))],
        out_shape=[
            jax.ShapeDtypeStruct((batch, length, pairs * LANES), BF16),
            jax.ShapeDtypeStruct((batch, length, columns), BF16),
        ],
        scratch_shapes=[pltpu.VMEM((length, LANES), BF16)] * 3
        + [pltpu.VMEM((length, LANES), F32)] * 3,
        compiler_params=pltpu.CompilerParams(vmem_limit_bytes=48 * 1024 * 1024),
        cost_estimate=pl.CostEstimate(
            flops=area * 2 * LANES * 7, bytes_accessed=batch * length * 4096, transcendentals=area
        ),
        name="attention",
    )(
        *([heads_pre] * 3),
        *([heads_bias.reshape(1, columns)] * 3),
        jnp.asarray(keep),
        jnp.asarray(below),
        jnp.asarray(above),
        segment_rows[:, :, None],
        segment_rows[:, None, :],
        attended_grad,
    )


def exact_pieces(vector):
    first = lax.reduce_precision(vector, 8, 7)
    rest = vector - first
    second = lax.reduce_precision(rest, 8, 7)
    third = rest - second
    return [piece.astype(BF16) for piece in (first, second, third)]


def on_device(
    block_input,
    attention_gain,
    attention_shift,
    feedforward_gain,
    feedforward_shift,
    projection,
    projection_bias,
    mixing,
    mixing_bias,
    expansion,
    expansion_bias,
    reduction,
    reduction_bias,
    segments,
    cotangent,
):
    local_width = projection.shape[0]
    heads_width = projection.shape[2]
    hidden_width = expansion.shape[1]
    tensor_rank = lax.axis_index("tensor")
    tensor_size = lax.axis_size("tensor")
    data_size = lax.axis_size("dp")
    width = local_width * data_size
    batch, rows = block_input.shape[0], block_input.shape[1]
    length = rows * tensor_size
    tokens = batch * length

    def across(data, distance):
        pairs = [(rank, rank ^ distance) for rank in range(tensor_size)]
        return lax.ppermute(data, "tensor", pairs)

    far = tensor_size // 2

    def gather_tokens(data):
        blocks = {0: data}
        distance = far
        while distance >= 1:
            for offset in list(blocks):
                blocks[offset ^ distance] = across(blocks[offset], distance)
            distance //= 2
        whole = jnp.zeros((batch, length) + data.shape[2:], data.dtype)
        for offset, block in blocks.items():
            whole = lax.dynamic_update_slice_in_dim(
                whole, block, (tensor_rank ^ offset) * rows, 1
            )
        return whole

    def scatter_tokens(whole):
        offsets = list(range(tensor_size))
        blocks = {
            offset: lax.dynamic_slice_in_dim(whole, (tensor_rank ^ offset) * rows, rows, 1)
            for offset in offsets
        }
        distance = 1
        while distance < tensor_size:
            kept = {}
            for offset in sorted(blocks, reverse=True):
                if offset & distance:
                    kept[offset ^ distance] = across(blocks[offset].astype(BF16), distance)
            blocks = {
                offset: blocks[offset].astype(F32) + kept[offset].astype(F32) for offset in kept
            }
            distance *= 2
        return blocks[0]

    vectors = [
        attention_gain,
        attention_shift,
        feedforward_gain,
        feedforward_shift,
        mixing_bias + reduction_bias,
        *[projection_bias[j] for j in range(3)],
        *[expansion_bias.reshape(-1, local_width)[j] for j in range(expansion_bias.shape[0] // local_width)],
    ]
    count = len(vectors)
    pieces = [piece for vector in vectors for piece in exact_pieces(vector)]
    packed = jnp.stack(pieces, axis=1)
    packed = jnp.pad(packed, ((0, 0), (0, LANES - packed.shape[1])))
    wide = lax.all_gather(
        jnp.concatenate([expansion, packed], axis=1), "dp", axis=0, tiled=True
    )
    expansion_all = wide[:, :hidden_width]
    small = wide[:, hidden_width : hidden_width + 3 * count].astype(F32)
    small = jnp.sum(small.reshape(width, count, 3), axis=2).T
    gain_attention, shift_attention, gain_feedforward, shift_feedforward, output_bias = [
        small[j] for j in range(5)
    ]
    heads_bias = lax.dynamic_slice_in_dim(small[5:8], tensor_rank * heads_width, heads_width, 1)
    hidden_bias_all = small[8:].reshape(-1, data_size, local_width).transpose(1, 0, 2).reshape(-1)
    hidden_bias = lax.dynamic_slice_in_dim(
        hidden_bias_all, tensor_rank * hidden_width, hidden_width, 0
    )
    reduction_all = lax.all_gather(reduction.T, "dp", axis=0, tiled=True)
    heads_weights = lax.all_gather(
        jnp.concatenate([projection.reshape(local_width, 3 * heads_width), mixing.T], axis=1),
        "dp",
        axis=0,
        tiled=True,
    )
    projection_all = heads_weights[:, : 3 * heads_width]
    mixing_all = heads_weights[:, 3 * heads_width :]

    inputs_all = gather_tokens(block_input).reshape(tokens, width)
    cotangent_all = gather_tokens(cotangent).reshape(tokens, width)
    segment_rows = gather_tokens(segments)

    def unit_of(data):
        values = data.astype(F32)
        average = jnp.mean(values, axis=-1, keepdims=True)
        centered = values - average
        variance = jnp.mean(centered * centered, axis=-1, keepdims=True)
        scale = lax.rsqrt(variance + EPS)
        return centered * scale, scale

    unit, _ = unit_of(inputs_all)
    first = (unit * gain_attention + shift_attention).astype(BF16)
    second = (unit * gain_feedforward + shift_feedforward).astype(BF16)

    hidden_pre = dot(second, expansion_all, 1, 0) + hidden_bias
    cumulative = 0.5 * (1.0 + lax.erf(hidden_pre * np.float32(0.5**0.5)))
    density = jnp.exp(-0.5 * hidden_pre * hidden_pre) * np.float32((2.0 * np.pi) ** -0.5)
    activated = (hidden_pre * cumulative).astype(BF16)
    activated_grad = dot(cotangent_all, reduction_all, 1, 0)
    hidden_grad = (activated_grad * (cumulative + hidden_pre * density)).astype(BF16)
    expansion_part = dot(second, hidden_grad, 0, 0)
    reduction_part = dot(cotangent_all, activated, 0, 0)
    hidden_sums = lax.psum_scatter(
        jnp.concatenate([expansion_part.astype(BF16), reduction_part.astype(BF16)], axis=1),
        "dp",
        scatter_dimension=0,
        tiled=True,
    )

    heads_pre = dot(first, projection_all, 1, 0).reshape(batch, length, 3 * heads_width)
    attended_grad = dot(cotangent_all, mixing_all, 1, 0).astype(BF16)
    attended, heads_grad = attention(
        heads_pre, heads_bias, segment_rows, attended_grad.reshape(batch, length, heads_width)
    )
    attended = attended.reshape(tokens, heads_width)
    heads_grad = heads_grad.reshape(tokens, 3 * heads_width)
    projection_part = dot(first, heads_grad, 0, 0)
    mixing_part = dot(cotangent_all, attended, 0, 0)
    heads_sums = lax.psum_scatter(
        jnp.concatenate([projection_part.astype(BF16), mixing_part.astype(BF16)], axis=1),
        "dp",
        scatter_dimension=0,
        tiled=True,
    )

    branch = dot(attended, mixing_all, 1, 1) + dot(activated, reduction_all, 1, 1)
    branch_rows = scatter_tokens(branch.astype(BF16).reshape(batch, length, width))
    local_input = block_input.astype(F32)
    block_output = (local_input + branch_rows + output_bias).astype(BF16)
    scaled = gain_attention * dot(heads_grad, projection_all, 1, 1)
    scaled = scaled + gain_feedforward * dot(hidden_grad, expansion_all, 1, 1)
    scaled_rows = scatter_tokens(scaled.astype(BF16).reshape(batch, length, width))
    local_unit, local_scale = unit_of(block_input)
    cotangent_rows = cotangent.astype(F32)
    input_gradient = (
        cotangent_rows
        + local_scale
        * (
            scaled_rows
            - jnp.mean(scaled_rows, axis=-1, keepdims=True)
            - local_unit * jnp.mean(scaled_rows * local_unit, axis=-1, keepdims=True)
        )
    ).astype(BF16)

    heads_sum = jnp.sum(heads_grad, axis=0, dtype=F32)
    hidden_sum = jnp.sum(hidden_grad, axis=0, dtype=F32)

    def norm_sums(weights, part, totals, gain, shift):
        shift_sum = jnp.sum(weights.astype(F32) * totals, axis=1)
        gain_sum = jnp.sum(weights.astype(F32) * part, axis=1)
        return (gain_sum - shift * shift_sum) / gain, shift_sum

    gain_a, shift_a = norm_sums(
        projection_all, projection_part, heads_sum, gain_attention, shift_attention
    )
    gain_f, shift_f = norm_sums(
        expansion_all, expansion_part, hidden_sum, gain_feedforward, shift_feedforward
    )
    cotangent_sum = jnp.sum(cotangent, axis=(0, 1), dtype=F32)
    heads_sums_wide = lax.dynamic_update_slice_in_dim(
        jnp.zeros((3, width), F32),
        heads_sum.reshape(3, heads_width),
        tensor_rank * heads_width,
        1,
    )
    hidden_sums_wide = lax.dynamic_update_slice_in_dim(
        jnp.zeros((hidden_width * tensor_size,), F32), hidden_sum, tensor_rank * hidden_width, 0
    )
    stacked = jnp.concatenate(
        [
            jnp.stack([gain_a, shift_a, gain_f, shift_f, cotangent_sum]).reshape(
                5, data_size, local_width
            ),
            heads_sums_wide.reshape(3, data_size, local_width),
            hidden_sums_wide.reshape(data_size, -1, local_width).transpose(1, 0, 2),
        ],
        axis=0,
    ).transpose(1, 0, 2)
    totals = lax.psum_scatter(
        stacked.reshape(data_size, -1), "dp", scatter_dimension=0, tiled=True
    )
    distance = 1
    while distance < tensor_size:
        totals = totals + across(totals, distance)
        distance *= 2
    totals = totals.reshape(-1, local_width)

    hidden_sums = hidden_sums.astype(F32)
    heads_sums = heads_sums.astype(F32)
    output_bias_gradient = totals[4]
    return (
        block_output,
        input_gradient,
        heads_sums[:, : 3 * heads_width].reshape(local_width, 3, heads_width),
        totals[5:8],
        heads_sums[:, 3 * heads_width :].T,
        output_bias_gradient,
        hidden_sums[:, :hidden_width],
        totals[8:].reshape(-1),
        hidden_sums[:, hidden_width:].T,
        output_bias_gradient,
        totals[0],
        totals[1],
        totals[2],
        totals[3],
    )


def solution(mesh):
    return jax.shard_map(
        on_device,
        mesh=mesh,
        in_specs=(
            P("dp", "tensor", None),
            P("dp"),
            P("dp"),
            P("dp"),
            P("dp"),
            P("dp", None, "tensor"),
            P(None, "dp"),
            P("tensor", "dp"),
            P("dp"),
            P("dp", "tensor"),
            P("dp"),
            P("tensor", "dp"),
            P("dp"),
            P("dp", "tensor"),
            P("dp", "tensor", None),
        ),
        out_specs=(
            P("dp", "tensor", None),
            P("dp", "tensor", None),
            P("dp", None, "tensor"),
            P(None, "dp"),
            P("tensor", "dp"),
            P("dp"),
            P("dp", "tensor"),
            P("dp"),
            P("tensor", "dp"),
            P("dp"),
            P("dp"),
            P("dp"),
            P("dp"),
            P("dp"),
        ),
        check_vma=False,
    )
```

```python
import numpy as np

import jax
import jax.numpy as jnp
from jax import lax
from jax.experimental import pallas as pl
from jax.experimental.pallas import tpu as pltpu
from jax.sharding import PartitionSpec as P

HD = 64
LANES = 128
EPS = 1e-05
MASKED = -1e30
F32 = jnp.float32
BF16 = jnp.bfloat16


def dot(left, right, left_dim, right_dim):
    return lax.dot_general(
        left, right, (((left_dim,), (right_dim,)), ((), ())), preferred_element_type=F32
    )


def rotary_lanes(length):
    half = HD // 8
    freqs = 1.0 / 10000.0 ** (np.arange(half, dtype=np.float32) * 2.0 / (2 * half))
    angles = np.arange(length, dtype=np.float32)[:, None] * freqs.astype(np.float32)[None, :]
    angles = angles.astype(np.float64)
    keep = np.ones((length, LANES), np.float32)
    from_below = np.zeros((length, LANES), np.float32)
    from_above = np.zeros((length, LANES), np.float32)
    for start in range(0, LANES, HD):
        keep[:, start : start + half] = np.cos(angles)
        keep[:, start + half : start + 2 * half] = np.cos(angles)
        from_above[:, start : start + half] = -np.sin(angles)
        from_below[:, start + half : start + 2 * half] = np.sin(angles)
    return keep, from_below, from_above


def attention_kernel(
    query_ref,
    key_ref,
    value_ref,
    query_bias,
    key_bias,
    value_bias,
    keep_ref,
    below_ref,
    above_ref,
    segment_column,
    segment_row,
    grad_ref,
    out_ref,
    heads_grad_ref,
    queries,
    keys,
    values,
    query_sum,
    key_sum,
    value_sum,
):
    length = query_ref.shape[1]
    block = min(256, length)
    half = HD // 8
    scale = HD**-0.5
    pair = pl.program_id(1)
    pair_count = pl.num_programs(1)

    def turn(data, sign):
        mixed = pltpu.roll(data, half, 1) * below_ref[...]
        mixed = mixed + pltpu.roll(data, LANES - half, 1) * above_ref[...]
        return data * keep_ref[...] + sign * mixed

    queries[...] = (turn(query_ref[0] + query_bias[...], 1.0)).astype(BF16) * BF16(scale)
    keys[...] = turn(key_ref[0] + key_bias[...], 1.0).astype(BF16)
    values[...] = (value_ref[0] + value_bias[...]).astype(BF16)
    key_sum[...] = jnp.zeros_like(key_sum)
    value_sum[...] = jnp.zeros_like(value_sum)
    for begin in range(0, length, block):
        stop = begin + block
        rows = lax.broadcasted_iota(jnp.int32, (block, stop), 0) + begin
        columns = lax.broadcasted_iota(jnp.int32, (block, stop), 1)
        allowed = (columns <= rows) & (
            segment_column[0, begin:stop, :] == segment_row[0, :, :stop]
        )
        out_block = jnp.zeros((block, LANES), F32)
        query_block = jnp.zeros((block, LANES), F32)
        for head in range(LANES // HD):

            def own(data):
                lane = lax.broadcasted_iota(jnp.int32, data.shape, 1)
                inside = (lane >= head * HD) & (lane < (head + 1) * HD)
                return jnp.where(inside, data.astype(F32), 0.0).astype(BF16)

            query = own(queries[begin:stop, :])
            grad = own(grad_ref[0, begin:stop, :])
            scores = jnp.where(allowed, dot(query, keys[:stop, :], 1, 1), MASKED)
            largest = jnp.max(scores, axis=1, keepdims=True)
            exponent = jnp.exp(scores - largest)
            probs = exponent * (1.0 / jnp.sum(exponent, axis=1, keepdims=True))
            rounded = probs.astype(BF16)
            out_block = out_block + dot(rounded, own(values[:stop, :]), 1, 0)
            prob_grad = dot(grad, values[:stop, :], 1, 1)
            delta = jnp.sum(prob_grad * probs, axis=1, keepdims=True)
            score_grad = (probs * (prob_grad - delta)).astype(BF16)
            query_block = query_block + dot(score_grad, own(keys[:stop, :]), 1, 0)
            key_sum[:stop, :] += dot(score_grad, query, 0, 0)
            value_sum[:stop, :] += dot(rounded, grad, 0, 0)
        out_ref[0, begin:stop, :] = out_block.astype(BF16)
        query_sum[begin:stop, :] = query_block * scale
    width = pair_count * LANES

    def place(index):
        return pl.ds(pl.multiple_of(index * width + pair * LANES, LANES), LANES)

    heads_grad_ref[0, :, place(0)] = turn(query_sum[...], -1.0).astype(BF16)
    heads_grad_ref[0, :, place(1)] = turn(key_sum[...], -1.0).astype(BF16)
    heads_grad_ref[0, :, place(2)] = value_sum[...].astype(BF16)


def attention(heads_pre, heads_bias, segment_rows, attended_grad):
    batch, length, columns = heads_pre.shape
    pairs = columns // (3 * LANES)
    keep, below, above = rotary_lanes(length)

    def part(index):
        return pl.BlockSpec((1, length, LANES), lambda b, p: (b, 0, index * pairs + p))

    def bias_part(index):
        return pl.BlockSpec((1, LANES), lambda b, p: (0, index * pairs + p))

    table = pl.BlockSpec((length, LANES), lambda b, p: (0, 0))
    piece = pl.BlockSpec((1, length, LANES), lambda b, p: (b, 0, p))
    area = batch * pairs * 2 * length * length * 5 // 8
    return pl.pallas_call(
        attention_kernel,
        grid=(batch, pairs),
        in_specs=[part(0), part(1), part(2), bias_part(0), bias_part(1), bias_part(2)]
        + [table] * 3
        + [
            pl.BlockSpec((1, length, 1), lambda b, p: (b, 0, 0)),
            pl.BlockSpec((1, 1, length), lambda b, p: (b, 0, 0)),
            piece,
        ],
        out_specs=[piece, pl.BlockSpec((1, length, columns), lambda b, p: (b, 0, 0))],
        out_shape=[
            jax.ShapeDtypeStruct((batch, length, pairs * LANES), BF16),
            jax.ShapeDtypeStruct((batch, length, columns), BF16),
        ],
        scratch_shapes=[pltpu.VMEM((length, LANES), BF16)] * 3
        + [pltpu.VMEM((length, LANES), F32)] * 3,
        compiler_params=pltpu.CompilerParams(vmem_limit_bytes=48 * 1024 * 1024),
        cost_estimate=pl.CostEstimate(
            flops=area * 2 * LANES * 28, bytes_accessed=batch * length * 4096, transcendentals=area
        ),
        name="attention",
    )(
        *([heads_pre] * 3),
        *([heads_bias.reshape(1, columns)] * 3),
        jnp.asarray(keep),
        jnp.asarray(below),
        jnp.asarray(above),
        segment_rows[:, :, None],
        segment_rows[:, None, :],
        attended_grad,
    )


def exact_pieces(vector):
    first = lax.reduce_precision(vector, 8, 7)
    rest = vector - first
    second = lax.reduce_precision(rest, 8, 7)
    third = rest - second
    return [piece.astype(BF16) for piece in (first, second, third)]


def on_device(
    block_input,
    attention_gain,
    attention_shift,
    feedforward_gain,
    feedforward_shift,
    projection,
    projection_bias,
    mixing,
    mixing_bias,
    expansion,
    expansion_bias,
    reduction,
    reduction_bias,
    segments,
    cotangent,
):
    local_width = projection.shape[0]
    heads_width = projection.shape[2]
    hidden_width = expansion.shape[1]
    tensor_rank = lax.axis_index("tensor")
    tensor_size = lax.axis_size("tensor")
    data_size = lax.axis_size("dp")
    width = local_width * data_size
    batch, rows = block_input.shape[0], block_input.shape[1]
    length = rows * tensor_size
    tokens = batch * length

    def across(data, distance):
        pairs = [(rank, rank ^ distance) for rank in range(tensor_size)]
        return lax.ppermute(data, "tensor", pairs)

    far = tensor_size // 2

    def gather_tokens(data):
        blocks = {0: data}
        distance = far
        while distance >= 1:
            for offset in list(blocks):
                blocks[offset ^ distance] = across(blocks[offset], distance)
            distance //= 2
        whole = jnp.zeros((batch, length) + data.shape[2:], data.dtype)
        for offset, block in blocks.items():
            whole = lax.dynamic_update_slice_in_dim(
                whole, block, (tensor_rank ^ offset) * rows, 1
            )
        return whole

    def scatter_tokens(whole):
        offsets = list(range(tensor_size))
        blocks = {
            offset: lax.dynamic_slice_in_dim(whole, (tensor_rank ^ offset) * rows, rows, 1)
            for offset in offsets
        }
        distance = 1
        while distance < tensor_size:
            kept = {}
            for offset in sorted(blocks, reverse=True):
                if offset & distance:
                    kept[offset ^ distance] = across(blocks[offset].astype(BF16), distance)
            blocks = {
                offset: blocks[offset].astype(F32) + kept[offset].astype(F32) for offset in kept
            }
            distance *= 2
        return blocks[0]

    data_rank = lax.axis_index("dp")
    halvings = [1]
    distance = data_size // 2
    while distance >= 2:
        halvings.append(distance)
        distance //= 2

    def across_data(data, distance):
        pairs = [(rank, rank ^ distance) for rank in range(data_size)]
        return lax.ppermute(data, "dp", pairs)

    def gather_data(block):
        held = {0: block}
        for distance in reversed(halvings):
            offsets = sorted(held)
            received = across_data(jnp.stack([held[offset] for offset in offsets]), distance)
            for place, offset in enumerate(offsets):
                held[offset ^ distance] = received[place]
        whole = jnp.zeros((data_size,) + block.shape, block.dtype)
        for offset, piece in held.items():
            whole = lax.dynamic_update_slice_in_dim(whole, piece[None], data_rank ^ offset, 0)
        return whole.reshape((data_size * block.shape[0],) + block.shape[1:])

    def scatter_data(whole, kind):
        blocks = {
            offset: lax.dynamic_index_in_dim(whole, data_rank ^ offset, 0, keepdims=False)
            for offset in range(data_size)
        }
        for distance in halvings:
            moving = [offset for offset in sorted(blocks) if offset & distance]
            sent = jnp.stack([blocks[offset].astype(kind) for offset in moving])
            received = across_data(sent, distance)
            blocks = {
                offset ^ distance: blocks[offset ^ distance] + received[place].astype(F32)
                for place, offset in enumerate(moving)
            }
        return blocks[0]

    vectors = [
        attention_gain,
        attention_shift,
        feedforward_gain,
        feedforward_shift,
        mixing_bias + reduction_bias,
        *[projection_bias[j] for j in range(3)],
        *[expansion_bias.reshape(-1, local_width)[j] for j in range(expansion_bias.shape[0] // local_width)],
    ]
    count = len(vectors)
    pieces = [piece for vector in vectors for piece in exact_pieces(vector)]
    packed = jnp.stack(pieces, axis=1)
    packed = jnp.pad(packed, ((0, 0), (0, LANES - packed.shape[1])))
    wide = lax.all_gather(
        jnp.concatenate([expansion, packed], axis=1), "dp", axis=0, tiled=True
    )
    expansion_all = wide[:, :hidden_width]
    small = wide[:, hidden_width : hidden_width + 3 * count].astype(F32)
    small = jnp.sum(small.reshape(width, count, 3), axis=2).T
    gain_attention, shift_attention, gain_feedforward, shift_feedforward, output_bias = [
        small[j] for j in range(5)
    ]
    heads_bias = lax.dynamic_slice_in_dim(small[5:8], tensor_rank * heads_width, heads_width, 1)
    hidden_bias_all = small[8:].reshape(-1, data_size, local_width).transpose(1, 0, 2).reshape(-1)
    hidden_bias = lax.dynamic_slice_in_dim(
        hidden_bias_all, tensor_rank * hidden_width, hidden_width, 0
    )
    reduction_all = gather_data(reduction.T)
    heads_local = jnp.concatenate(
        [projection.reshape(local_width, 3 * heads_width), mixing.T], axis=1
    )
    heads_local, wide = lax.optimization_barrier((heads_local, wide))
    heads_weights = lax.all_gather(
        heads_local,
        "dp",
        axis=0,
        tiled=True,
    )
    projection_all = heads_weights[:, : 3 * heads_width]
    mixing_all = heads_weights[:, 3 * heads_width :]

    inputs_all = gather_tokens(block_input).reshape(tokens, width)
    cotangent_all = gather_tokens(cotangent).reshape(tokens, width)
    segment_rows = gather_tokens(segments)

    def unit_of(data):
        values = data.astype(F32)
        average = jnp.mean(values, axis=-1, keepdims=True)
        centered = values - average
        variance = jnp.mean(centered * centered, axis=-1, keepdims=True)
        scale = lax.rsqrt(variance + EPS)
        return centered * scale, scale

    unit, _ = unit_of(inputs_all)
    first = (unit * gain_attention + shift_attention).astype(BF16)
    second = (unit * gain_feedforward + shift_feedforward).astype(BF16)

    hidden_pre = dot(second, expansion_all, 1, 0) + hidden_bias
    cumulative = 0.5 * (1.0 + lax.erf(hidden_pre * np.float32(0.5**0.5)))
    density = jnp.exp(-0.5 * hidden_pre * hidden_pre) * np.float32((2.0 * np.pi) ** -0.5)
    activated = (hidden_pre * cumulative).astype(BF16)
    activated_grad = dot(cotangent_all, reduction_all, 1, 0)
    hidden_grad = (activated_grad * (cumulative + hidden_pre * density)).astype(BF16)
    expansion_part = dot(second, hidden_grad, 0, 0)
    reduction_part = dot(cotangent_all, activated, 0, 0)
    by_rank = (data_size, local_width, hidden_width)
    hidden_sums = lax.psum_scatter(
        jnp.concatenate(
            [
                expansion_part.astype(BF16).reshape(by_rank),
                reduction_part.astype(BF16).reshape(by_rank),
            ],
            axis=1,
        ),
        "dp",
        scatter_dimension=0,
        tiled=True,
    )

    heads_pre = dot(first, projection_all, 1, 0).reshape(batch, length, 3 * heads_width)
    attended_grad = dot(cotangent_all, mixing_all, 1, 0).astype(BF16)
    attended_grad = attended_grad.reshape(batch, length, heads_width)
    hidden_branch = dot(activated, reduction_all, 1, 1)
    hidden_scaled = gain_feedforward * dot(hidden_grad, expansion_all, 1, 1)
    projection_part = mixing_part = heads_sum = 0.0
    branch_rows, scaled_rows = [], []
    for index in range(batch):
        part = slice(index, index + 1)
        own_rows = slice(index * length, (index + 1) * length)
        grad_part = attended_grad[part]
        if index:
            grad_part, branch_rows[-1], scaled_rows[-1] = lax.optimization_barrier(
                (grad_part, branch, scaled)
            )
            branch_rows[-1] = scatter_tokens(branch_rows[-1])
            scaled_rows[-1] = scatter_tokens(scaled_rows[-1])
        attended, heads_grad = attention(
            heads_pre[part], heads_bias, segment_rows[part], grad_part
        )
        attended, heads_grad = attended[0], heads_grad[0]
        branch = hidden_branch[own_rows] + dot(attended, mixing_all, 1, 1)
        branch = branch.astype(BF16)[None]
        branch_rows.append(branch)
        scaled = hidden_scaled[own_rows] + gain_attention * dot(heads_grad, projection_all, 1, 1)
        scaled = scaled.astype(BF16)[None]
        scaled_rows.append(scaled)
        projection_part = projection_part + dot(first[own_rows], heads_grad, 0, 0)
        mixing_part = mixing_part + dot(cotangent_all[own_rows], attended, 0, 0)
        heads_sum = heads_sum + jnp.sum(heads_grad, axis=0, dtype=F32)
    branch_rows[-1] = scatter_tokens(branch_rows[-1])
    scaled_rows[-1] = scatter_tokens(scaled_rows[-1])
    branch_rows = jnp.concatenate(branch_rows, axis=0)
    scaled_rows = jnp.concatenate(scaled_rows, axis=0)
    projection_sums = scatter_data(
        projection_part.reshape(data_size, local_width, 3 * heads_width), BF16
    )
    mixing_sums = scatter_data(mixing_part.reshape(data_size, local_width, heads_width), BF16)

    local_input = block_input.astype(F32)
    block_output = (local_input + branch_rows + output_bias).astype(BF16)
    local_unit, local_scale = unit_of(block_input)
    cotangent_rows = cotangent.astype(F32)
    input_gradient = (
        cotangent_rows
        + local_scale
        * (
            scaled_rows
            - jnp.mean(scaled_rows, axis=-1, keepdims=True)
            - local_unit * jnp.mean(scaled_rows * local_unit, axis=-1, keepdims=True)
        )
    ).astype(BF16)

    hidden_sum = jnp.sum(hidden_grad, axis=0, dtype=F32)

    def norm_sums(weights, part, totals, gain, shift):
        shift_sum = jnp.sum(weights.astype(F32) * totals, axis=1)
        gain_sum = jnp.sum(weights.astype(F32) * part, axis=1)
        return (gain_sum - shift * shift_sum) / gain, shift_sum

    gain_a, shift_a = norm_sums(
        projection_all, projection_part, heads_sum, gain_attention, shift_attention
    )
    gain_f, shift_f = norm_sums(
        expansion_all, expansion_part, hidden_sum, gain_feedforward, shift_feedforward
    )
    cotangent_sum = jnp.sum(cotangent, axis=(0, 1), dtype=F32)
    heads_sums_wide = lax.dynamic_update_slice_in_dim(
        jnp.zeros((3, width), F32),
        heads_sum.reshape(3, heads_width),
        tensor_rank * heads_width,
        1,
    )
    hidden_sums_wide = lax.dynamic_update_slice_in_dim(
        jnp.zeros((hidden_width * tensor_size,), F32), hidden_sum, tensor_rank * hidden_width, 0
    )
    stacked = jnp.concatenate(
        [
            jnp.stack([gain_a, shift_a, gain_f, shift_f, cotangent_sum]).reshape(
                5, data_size, local_width
            ),
            heads_sums_wide.reshape(3, data_size, local_width),
            hidden_sums_wide.reshape(data_size, -1, local_width).transpose(1, 0, 2),
        ],
        axis=0,
    ).transpose(1, 0, 2)
    totals = scatter_data(stacked.reshape(data_size, -1), F32)
    distance = 1
    while distance < tensor_size:
        totals = totals + across(totals, distance)
        distance *= 2
    totals = totals.reshape(-1, local_width)

    hidden_sums = hidden_sums.reshape(2, local_width, hidden_width).astype(F32)
    output_bias_gradient = totals[4]
    return (
        block_output,
        input_gradient,
        projection_sums.reshape(local_width, 3, heads_width),
        totals[5:8],
        mixing_sums.T,
        output_bias_gradient,
        hidden_sums[0],
        totals[8:].reshape(-1),
        hidden_sums[1].T,
        output_bias_gradient,
        totals[0],
        totals[1],
        totals[2],
        totals[3],
    )


def solution(mesh):
    return jax.shard_map(
        on_device,
        mesh=mesh,
        in_specs=(
            P("dp", "tensor", None),
            P("dp"),
            P("dp"),
            P("dp"),
            P("dp"),
            P("dp", None, "tensor"),
            P(None, "dp"),
            P("tensor", "dp"),
            P("dp"),
            P("dp", "tensor"),
            P("dp"),
            P("tensor", "dp"),
            P("dp"),
            P("dp", "tensor"),
            P("dp", "tensor", None),
        ),
        out_specs=(
            P("dp", "tensor", None),
            P("dp", "tensor", None),
            P("dp", None, "tensor"),
            P(None, "dp"),
            P("tensor", "dp"),
            P("dp"),
            P("dp", "tensor"),
            P("dp"),
            P("tensor", "dp"),
            P("dp"),
            P("dp"),
            P("dp"),
            P("dp"),
            P("dp"),
        ),
        check_vma=False,
    )
```

```python
import numpy as np

import jax
import jax.numpy as jnp
from jax import lax
from jax.experimental import pallas as pl
from jax.experimental.pallas import tpu as pltpu
from jax.sharding import PartitionSpec as P

HD = 64
LANES = 128
EPS = 1e-05
MASKED = -1e30
F32 = jnp.float32
BF16 = jnp.bfloat16


def dot(left, right, left_dim, right_dim):
    return lax.dot_general(
        left, right, (((left_dim,), (right_dim,)), ((), ())), preferred_element_type=F32
    )


def rotary_lanes(length):
    half = HD // 8
    freqs = 1.0 / 10000.0 ** (np.arange(half, dtype=np.float32) * 2.0 / (2 * half))
    angles = np.arange(length, dtype=np.float32)[:, None] * freqs.astype(np.float32)[None, :]
    angles = angles.astype(np.float64)
    keep = np.ones((length, LANES), np.float32)
    from_below = np.zeros((length, LANES), np.float32)
    from_above = np.zeros((length, LANES), np.float32)
    for start in range(0, LANES, HD):
        keep[:, start : start + half] = np.cos(angles)
        keep[:, start + half : start + 2 * half] = np.cos(angles)
        from_above[:, start : start + half] = -np.sin(angles)
        from_below[:, start + half : start + 2 * half] = np.sin(angles)
    return keep, from_below, from_above


def attention_kernel(
    query_ref,
    key_ref,
    value_ref,
    query_bias,
    key_bias,
    value_bias,
    keep_ref,
    below_ref,
    above_ref,
    segment_column,
    segment_row,
    grad_ref,
    out_ref,
    heads_grad_ref,
    queries,
    keys,
    values,
    query_sum,
    key_sum,
    value_sum,
):
    length = query_ref.shape[1]
    block = min(256, length)
    half = HD // 8
    scale = HD**-0.5
    pair = pl.program_id(1)
    pair_count = pl.num_programs(1)

    def turn(data, sign):
        mixed = pltpu.roll(data, half, 1) * below_ref[...]
        mixed = mixed + pltpu.roll(data, LANES - half, 1) * above_ref[...]
        return data * keep_ref[...] + sign * mixed

    queries[...] = (turn(query_ref[0] + query_bias[...], 1.0)).astype(BF16) * BF16(scale)
    keys[...] = turn(key_ref[0] + key_bias[...], 1.0).astype(BF16)
    values[...] = (value_ref[0] + value_bias[...]).astype(BF16)
    key_sum[...] = jnp.zeros_like(key_sum)
    value_sum[...] = jnp.zeros_like(value_sum)
    for begin in range(0, length, block):
        stop = begin + block
        rows = lax.broadcasted_iota(jnp.int32, (block, stop), 0) + begin
        columns = lax.broadcasted_iota(jnp.int32, (block, stop), 1)
        allowed = (columns <= rows) & (
            segment_column[0, begin:stop, :] == segment_row[0, :, :stop]
        )
        out_block = jnp.zeros((block, LANES), F32)
        query_block = jnp.zeros((block, LANES), F32)
        for head in range(LANES // HD):

            def own(data):
                lane = lax.broadcasted_iota(jnp.int32, data.shape, 1)
                inside = (lane >= head * HD) & (lane < (head + 1) * HD)
                return jnp.where(inside, data.astype(F32), 0.0).astype(BF16)

            query = own(queries[begin:stop, :])
            grad = own(grad_ref[0, begin:stop, :])
            scores = jnp.where(allowed, dot(query, keys[:stop, :], 1, 1), MASKED)
            largest = jnp.max(scores, axis=1, keepdims=True)
            exponent = jnp.exp(scores - largest)
            probs = exponent * (1.0 / jnp.sum(exponent, axis=1, keepdims=True))
            rounded = probs.astype(BF16)
            out_block = out_block + dot(rounded, own(values[:stop, :]), 1, 0)
            prob_grad = dot(grad, values[:stop, :], 1, 1)
            delta = jnp.sum(prob_grad * probs, axis=1, keepdims=True)
            score_grad = (probs * (prob_grad - delta)).astype(BF16)
            query_block = query_block + dot(score_grad, own(keys[:stop, :]), 1, 0)
            key_sum[:stop, :] += dot(score_grad, query, 0, 0)
            value_sum[:stop, :] += dot(rounded, grad, 0, 0)
        out_ref[0, begin:stop, :] = out_block.astype(BF16)
        query_sum[begin:stop, :] = query_block * scale
    width = pair_count * LANES

    def place(index):
        return pl.ds(pl.multiple_of(index * width + pair * LANES, LANES), LANES)

    heads_grad_ref[0, :, place(0)] = turn(query_sum[...], -1.0).astype(BF16)
    heads_grad_ref[0, :, place(1)] = turn(key_sum[...], -1.0).astype(BF16)
    heads_grad_ref[0, :, place(2)] = value_sum[...].astype(BF16)


def attention(heads_pre, heads_bias, segment_rows, attended_grad):
    batch, length, columns = heads_pre.shape
    pairs = columns // (3 * LANES)
    keep, below, above = rotary_lanes(length)

    def part(index):
        return pl.BlockSpec((1, length, LANES), lambda b, p: (b, 0, index * pairs + p))

    def bias_part(index):
        return pl.BlockSpec((1, LANES), lambda b, p: (0, index * pairs + p))

    table = pl.BlockSpec((length, LANES), lambda b, p: (0, 0))
    piece = pl.BlockSpec((1, length, LANES), lambda b, p: (b, 0, p))
    area = batch * pairs * 2 * length * length * 5 // 8
    return pl.pallas_call(
        attention_kernel,
        grid=(batch, pairs),
        in_specs=[part(0), part(1), part(2), bias_part(0), bias_part(1), bias_part(2)]
        + [table] * 3
        + [
            pl.BlockSpec((1, length, 1), lambda b, p: (b, 0, 0)),
            pl.BlockSpec((1, 1, length), lambda b, p: (b, 0, 0)),
            piece,
        ],
        out_specs=[piece, pl.BlockSpec((1, length, columns), lambda b, p: (b, 0, 0))],
        out_shape=[
            jax.ShapeDtypeStruct((batch, length, pairs * LANES), BF16),
            jax.ShapeDtypeStruct((batch, length, columns), BF16),
        ],
        scratch_shapes=[pltpu.VMEM((length, LANES), BF16)] * 3
        + [pltpu.VMEM((length, LANES), F32)] * 3,
        compiler_params=pltpu.CompilerParams(vmem_limit_bytes=48 * 1024 * 1024),
        cost_estimate=pl.CostEstimate(
            flops=area * 2 * LANES * 28, bytes_accessed=batch * length * 4096, transcendentals=area
        ),
        name="attention",
    )(
        *([heads_pre] * 3),
        *([heads_bias.reshape(1, columns)] * 3),
        jnp.asarray(keep),
        jnp.asarray(below),
        jnp.asarray(above),
        segment_rows[:, :, None],
        segment_rows[:, None, :],
        attended_grad,
    )


def exact_pieces(vector):
    first = lax.reduce_precision(vector, 8, 7)
    rest = vector - first
    second = lax.reduce_precision(rest, 8, 7)
    third = rest - second
    return [piece.astype(BF16) for piece in (first, second, third)]


def on_device(
    block_input,
    attention_gain,
    attention_shift,
    feedforward_gain,
    feedforward_shift,
    projection,
    projection_bias,
    mixing,
    mixing_bias,
    expansion,
    expansion_bias,
    reduction,
    reduction_bias,
    segments,
    cotangent,
):
    local_width = projection.shape[0]
    heads_width = projection.shape[2]
    hidden_width = expansion.shape[1]
    tensor_rank = lax.axis_index("tensor")
    tensor_size = lax.axis_size("tensor")
    data_size = lax.axis_size("dp")
    width = local_width * data_size
    batch, rows = block_input.shape[0], block_input.shape[1]
    length = rows * tensor_size
    tokens = batch * length

    def across(data, distance):
        pairs = [(rank, rank ^ distance) for rank in range(tensor_size)]
        return lax.ppermute(data, "tensor", pairs)

    far = tensor_size // 2

    def gather_tokens(data):
        blocks = {0: data}
        distance = far
        while distance >= 1:
            for offset in list(blocks):
                blocks[offset ^ distance] = across(blocks[offset], distance)
            distance //= 2
        whole = jnp.zeros((batch, length) + data.shape[2:], data.dtype)
        for offset, block in blocks.items():
            whole = lax.dynamic_update_slice_in_dim(
                whole, block, (tensor_rank ^ offset) * rows, 1
            )
        return whole

    def scatter_tokens(whole):
        offsets = list(range(tensor_size))
        blocks = {
            offset: lax.dynamic_slice_in_dim(whole, (tensor_rank ^ offset) * rows, rows, 1)
            for offset in offsets
        }
        distance = 1
        while distance < tensor_size:
            kept = {}
            for offset in sorted(blocks, reverse=True):
                if offset & distance:
                    kept[offset ^ distance] = across(blocks[offset].astype(BF16), distance)
            blocks = {
                offset: blocks[offset].astype(F32) + kept[offset].astype(F32) for offset in kept
            }
            distance *= 2
        return blocks[0]

    data_rank = lax.axis_index("dp")
    halvings = [1]
    distance = data_size // 2
    while distance >= 2:
        halvings.append(distance)
        distance //= 2

    def across_data(data, distance):
        pairs = [(rank, rank ^ distance) for rank in range(data_size)]
        return lax.ppermute(data, "dp", pairs)

    def scatter_data(whole, kind):
        blocks = {
            offset: lax.dynamic_index_in_dim(whole, data_rank ^ offset, 0, keepdims=False)
            for offset in range(data_size)
        }
        for distance in halvings:
            moving = [offset for offset in sorted(blocks) if offset & distance]
            sent = jnp.stack([blocks[offset].astype(kind) for offset in moving])
            received = across_data(sent, distance)
            blocks = {
                offset ^ distance: blocks[offset ^ distance] + received[place].astype(F32)
                for place, offset in enumerate(moving)
            }
        return blocks[0]

    vectors = [
        attention_gain,
        attention_shift,
        feedforward_gain,
        feedforward_shift,
        mixing_bias + reduction_bias,
        *[projection_bias[j] for j in range(3)],
        *[expansion_bias.reshape(-1, local_width)[j] for j in range(expansion_bias.shape[0] // local_width)],
    ]
    count = len(vectors)
    pieces = [piece for vector in vectors for piece in exact_pieces(vector)]
    packed = jnp.stack(pieces, axis=1)
    packed = jnp.pad(packed, ((0, 0), (0, LANES - packed.shape[1])))
    columns = [
        expansion,
        packed,
        reduction.T,
        projection.reshape(local_width, 3 * heads_width),
        mixing.T,
    ]
    wide = lax.all_gather(jnp.concatenate(columns, axis=1), "dp", axis=0, tiled=True)
    edges = np.cumsum([0] + [column.shape[1] for column in columns])
    expansion_all, _, reduction_all, projection_all, mixing_all = [
        wide[:, edges[j] : edges[j + 1]] for j in range(len(columns))
    ]
    small = wide[:, hidden_width : hidden_width + 3 * count].astype(F32)
    small = jnp.sum(small.reshape(width, count, 3), axis=2).T
    gain_attention, shift_attention, gain_feedforward, shift_feedforward, output_bias = [
        small[j] for j in range(5)
    ]
    heads_bias = lax.dynamic_slice_in_dim(small[5:8], tensor_rank * heads_width, heads_width, 1)
    hidden_bias_all = small[8:].reshape(-1, data_size, local_width).transpose(1, 0, 2).reshape(-1)
    hidden_bias = lax.dynamic_slice_in_dim(
        hidden_bias_all, tensor_rank * hidden_width, hidden_width, 0
    )

    inputs_all = gather_tokens(block_input).reshape(tokens, width)
    cotangent_all = gather_tokens(cotangent).reshape(tokens, width)
    segment_rows = gather_tokens(segments)

    def unit_of(data):
        values = data.astype(F32)
        average = jnp.mean(values, axis=-1, keepdims=True)
        centered = values - average
        variance = jnp.mean(centered * centered, axis=-1, keepdims=True)
        scale = lax.rsqrt(variance + EPS)
        return centered * scale, scale

    unit, _ = unit_of(inputs_all)
    first = (unit * gain_attention + shift_attention).astype(BF16)
    second = (unit * gain_feedforward + shift_feedforward).astype(BF16)

    hidden_pre = dot(second, expansion_all, 1, 0) + hidden_bias
    cumulative = 0.5 * (1.0 + lax.erf(hidden_pre * np.float32(0.5**0.5)))
    density = jnp.exp(-0.5 * hidden_pre * hidden_pre) * np.float32((2.0 * np.pi) ** -0.5)
    activated = (hidden_pre * cumulative).astype(BF16)
    activated_grad = dot(cotangent_all, reduction_all, 1, 0)
    hidden_grad = (activated_grad * (cumulative + hidden_pre * density)).astype(BF16)
    expansion_part = dot(second, hidden_grad, 0, 0)
    reduction_part = dot(cotangent_all, activated, 0, 0)
    by_rank = (data_size, local_width, hidden_width)
    hidden_sums = lax.psum_scatter(
        jnp.concatenate(
            [
                expansion_part.astype(BF16).reshape(by_rank),
                reduction_part.astype(BF16).reshape(by_rank),
            ],
            axis=1,
        ),
        "dp",
        scatter_dimension=0,
        tiled=True,
    )

    heads_pre = dot(first, projection_all, 1, 0).reshape(batch, length, 3 * heads_width)
    attended_grad = dot(cotangent_all, mixing_all, 1, 0).astype(BF16)
    attended_grad = attended_grad.reshape(batch, length, heads_width)
    hidden_branch = dot(activated, reduction_all, 1, 1)
    hidden_scaled = gain_feedforward * dot(hidden_grad, expansion_all, 1, 1)
    projection_part = mixing_part = heads_sum = 0.0
    branch_rows, scaled_rows = [], []
    for index in range(batch):
        part = slice(index, index + 1)
        own_rows = slice(index * length, (index + 1) * length)
        grad_part = attended_grad[part]
        if index:
            grad_part, branch_rows[-1], scaled_rows[-1] = lax.optimization_barrier(
                (grad_part, branch, scaled)
            )
            branch_rows[-1] = scatter_tokens(branch_rows[-1])
            scaled_rows[-1] = scatter_tokens(scaled_rows[-1])
        attended, heads_grad = attention(
            heads_pre[part], heads_bias, segment_rows[part], grad_part
        )
        attended, heads_grad = attended[0], heads_grad[0]
        branch = hidden_branch[own_rows] + dot(attended, mixing_all, 1, 1)
        branch = branch.astype(BF16)[None]
        branch_rows.append(branch)
        scaled = hidden_scaled[own_rows] + gain_attention * dot(heads_grad, projection_all, 1, 1)
        scaled = scaled.astype(BF16)[None]
        scaled_rows.append(scaled)
        projection_part = projection_part + dot(first[own_rows], heads_grad, 0, 0)
        mixing_part = mixing_part + dot(cotangent_all[own_rows], attended, 0, 0)
        heads_sum = heads_sum + jnp.sum(heads_grad, axis=0, dtype=F32)
    branch_rows[-1] = scatter_tokens(branch_rows[-1])
    scaled_rows[-1] = scatter_tokens(scaled_rows[-1])
    branch_rows = jnp.concatenate(branch_rows, axis=0)
    scaled_rows = jnp.concatenate(scaled_rows, axis=0)
    heads_sums = lax.psum_scatter(
        jnp.concatenate([projection_part.astype(BF16), mixing_part.astype(BF16)], axis=1),
        "dp",
        scatter_dimension=0,
        tiled=True,
    ).astype(F32)

    local_input = block_input.astype(F32)
    block_output = (local_input + branch_rows + output_bias).astype(BF16)
    local_unit, local_scale = unit_of(block_input)
    cotangent_rows = cotangent.astype(F32)
    input_gradient = (
        cotangent_rows
        + local_scale
        * (
            scaled_rows
            - jnp.mean(scaled_rows, axis=-1, keepdims=True)
            - local_unit * jnp.mean(scaled_rows * local_unit, axis=-1, keepdims=True)
        )
    ).astype(BF16)

    hidden_sum = jnp.sum(hidden_grad, axis=0, dtype=F32)

    def norm_sums(weights, part, totals, gain, shift):
        shift_sum = jnp.sum(weights.astype(F32) * totals, axis=1)
        gain_sum = jnp.sum(weights.astype(F32) * part, axis=1)
        return (gain_sum - shift * shift_sum) / gain, shift_sum

    gain_a, shift_a = norm_sums(
        projection_all, projection_part, heads_sum, gain_attention, shift_attention
    )
    gain_f, shift_f = norm_sums(
        expansion_all, expansion_part, hidden_sum, gain_feedforward, shift_feedforward
    )
    cotangent_sum = jnp.sum(cotangent, axis=(0, 1), dtype=F32)
    heads_sums_wide = lax.dynamic_update_slice_in_dim(
        jnp.zeros((3, width), F32),
        heads_sum.reshape(3, heads_width),
        tensor_rank * heads_width,
        1,
    )
    hidden_sums_wide = lax.dynamic_update_slice_in_dim(
        jnp.zeros((hidden_width * tensor_size,), F32), hidden_sum, tensor_rank * hidden_width, 0
    )
    stacked = jnp.concatenate(
        [
            jnp.stack([gain_a, shift_a, gain_f, shift_f, cotangent_sum]).reshape(
                5, data_size, local_width
            ),
            heads_sums_wide.reshape(3, data_size, local_width),
            hidden_sums_wide.reshape(data_size, -1, local_width).transpose(1, 0, 2),
        ],
        axis=0,
    ).transpose(1, 0, 2)
    totals = scatter_data(stacked.reshape(data_size, -1), F32)
    distance = 1
    while distance < tensor_size:
        totals = totals + across(totals, distance)
        distance *= 2
    totals = totals.reshape(-1, local_width)

    hidden_sums = hidden_sums.reshape(2, local_width, hidden_width).astype(F32)
    output_bias_gradient = totals[4]
    return (
        block_output,
        input_gradient,
        heads_sums[:, : 3 * heads_width].reshape(local_width, 3, heads_width),
        totals[5:8],
        heads_sums[:, 3 * heads_width :].T,
        output_bias_gradient,
        hidden_sums[0],
        totals[8:].reshape(-1),
        hidden_sums[1].T,
        output_bias_gradient,
        totals[0],
        totals[1],
        totals[2],
        totals[3],
    )


def solution(mesh):
    return jax.shard_map(
        on_device,
        mesh=mesh,
        in_specs=(
            P("dp", "tensor", None),
            P("dp"),
            P("dp"),
            P("dp"),
            P("dp"),
            P("dp", None, "tensor"),
            P(None, "dp"),
            P("tensor", "dp"),
            P("dp"),
            P("dp", "tensor"),
            P("dp"),
            P("tensor", "dp"),
            P("dp"),
            P("dp", "tensor"),
            P("dp", "tensor", None),
        ),
        out_specs=(
            P("dp", "tensor", None),
            P("dp", "tensor", None),
            P("dp", None, "tensor"),
            P(None, "dp"),
            P("tensor", "dp"),
            P("dp"),
            P("dp", "tensor"),
            P("dp"),
            P("tensor", "dp"),
            P("dp"),
            P("dp"),
            P("dp"),
            P("dp"),
            P("dp"),
        ),
        check_vma=False,
    )
```
